32 devices in a mesh: dp: 4 (over x, core), seq: 8 (over z, y).
Axes of the slice: x: 2, y: 2, z: 4, core: 2. Of those that a mesh axis runs over, the one named last changes fastest.
Arguments:
- inputs: bfloat16 [4, 4096, 768], P('dp', 'seq'), may hold values from -6 to 6
- block_mix: bfloat16 [8, 512, 512], P('seq'), may hold values from -0.25 to 0.25
- cross_mix: bfloat16 [512, 8, 8], P('seq'), may hold values from -2 to 2
- cotangent: bfloat16 [4, 4096, 768], P('dp', 'seq'), may hold values from -0.59765625 to 0.59765625
Outputs:
- output: bfloat16 [4, 4096, 768], P('dp', 'seq')
- input_grad: bfloat16 [4, 4096, 768], P('dp', 'seq')
- block_grad: bfloat16 [8, 512, 512], P('seq')
- cross_grad: bfloat16 [512, 8, 8], P('seq')
The draws below stay inside these ranges and needn't reach their ends.
All inputs are finite; a program needn't handle non-finite values.
Results may differ from the reference program's by a relative error of at most 0.012.
Values may be sent and summed in bfloat16 or wider, within the bound.
A program may use at most 64 MiB of HBM per device.

```python
import jax
import jax.numpy as jnp
from jax import lax

C = 768
BS = 512
NB = 8
LEN = 4096
SEQS = 4


def block_levels(rng, extent, shards, smallest, high):
    gain = 1.0
    for axis_at, parts in shards:
        steps = jax.random.uniform(jax.random.fold_in(jax.random.fold_in(rng, 6), axis_at), (parts,), jnp.float32, smallest / len(shards), high / len(shards))
        gain = gain * jnp.repeat(jnp.exp(steps), extent[axis_at] // parts).reshape((-1,) + (1,) * (len(extent) - 1 - axis_at))
    return gain


def gaussian(rng, dims, scale, most, split=(), dtype=jnp.bfloat16):
    values = scale * jax.random.normal(rng, dims, jnp.float32)
    if split:
        values = values * block_levels(rng, dims, split, -0.22, 0.18)
    return jnp.clip(values, -most, most).astype(dtype)


def setup_inputs(seed: int = 0) -> dict:
    key_of = jax.random.split(jax.random.key(seed), 5)
    return {
        "inputs": gaussian(key_of[0], (SEQS, LEN, C), 1.0, 6.0, ((0, 4), (1, 8))),
        "block_mix": gaussian(key_of[1], (NB, BS, BS), BS ** -0.5, 0.25, ((0, 8),)),
        "cross_mix": gaussian(key_of[2], (BS, NB, NB), NB ** -0.5, 2.0, ((0, 8),)),
        "cotangent": gaussian(key_of[3], (SEQS, LEN, C), 0.1, 0.59765625, ((0, 4), (1, 8))),
    }


def one_sequence(pair, block_f, cross_f):
    inputs_one, cot_one = pair
    x = inputs_one.reshape(NB, BS, C)
    xf = x.astype(jnp.float32)
    h = jnp.einsum('bsr,brc->bsc', block_f, xf).astype(jnp.bfloat16)
    z = jnp.einsum('rab,brc->arc', cross_f, h.astype(jnp.float32)).astype(jnp.bfloat16)
    gate = jax.nn.sigmoid(xf)
    zf = z.astype(jnp.float32)
    out = (xf + zf * gate).astype(jnp.bfloat16)
    dyf = cot_one.reshape(NB, BS, C).astype(jnp.float32)
    dz = (dyf * gate).astype(jnp.bfloat16)
    dzf = dz.astype(jnp.float32)
    dh = jnp.einsum('rab,arc->brc', cross_f, dzf).astype(jnp.bfloat16)
    cross_part = jnp.einsum('arc,brc->rab', dzf, h.astype(jnp.float32))
    dhf = dh.astype(jnp.float32)
    dv = jnp.einsum('bsr,bsc->brc', block_f, dhf)
    block_part = jnp.einsum('bsc,brc->bsr', dhf, xf)
    dx = (dyf * (1.0 + zf * gate * (1.0 - gate)) + dv).astype(jnp.bfloat16)
    return out.reshape(LEN, C), dx.reshape(LEN, C), block_part, cross_part


def reference(inputs, block_mix, cross_mix, cotangent):
    block_f = block_mix.astype(jnp.float32)
    cross_f = cross_mix.astype(jnp.float32)
    outs, grads, block_parts, cross_parts = lax.map(
        lambda pair: one_sequence(pair, block_f, cross_f), (inputs, cotangent))
    block_grad = jnp.sum(block_parts, axis=0).astype(jnp.bfloat16)
    cross_grad = jnp.sum(cross_parts, axis=0).astype(jnp.bfloat16)
    return outs, grads, block_grad, cross_grad
```

```python
import functools

import jax
import jax.numpy as jnp
from jax import lax
from jax.experimental import pallas as pl
from jax.experimental.pallas import tpu as pltpu
from jax.sharding import PartitionSpec as P

MESH = pl.DeviceIdType.MESH
BF16, F32 = jnp.bfloat16, jnp.float32


def plain(inputs, block_mix, cross_mix, cotangent):
    h = jnp.einsum("bsr,brc->bsc", block_mix, inputs, preferred_element_type=jnp.float32).astype(
        jnp.bfloat16
    )
    gate = jax.nn.sigmoid(inputs.astype(jnp.float32))
    h_cols = lax.all_to_all(h, "seq", split_axis=1, concat_axis=0, tiled=True)
    z_cols = jnp.einsum(
        "rab,brc->arc", cross_mix, h_cols, preferred_element_type=jnp.float32
    ).astype(jnp.bfloat16)
    z = lax.all_to_all(z_cols, "seq", split_axis=0, concat_axis=1, tiled=True)
    dz = (cotangent.astype(jnp.float32) * gate).astype(jnp.bfloat16)
    dz_cols = lax.all_to_all(dz, "seq", split_axis=1, concat_axis=0, tiled=True)
    dh_cols = jnp.einsum(
        "rab,arc->brc", cross_mix, dz_cols, preferred_element_type=jnp.float32
    ).astype(jnp.bfloat16)
    cross_part = jnp.einsum("arc,brc->rab", dz_cols, h_cols, preferred_element_type=jnp.float32)
    dh = lax.all_to_all(dh_cols, "seq", split_axis=0, concat_axis=1, tiled=True)
    dv = jnp.einsum("bsr,bsc->brc", block_mix, dh, preferred_element_type=jnp.float32)
    block_part = jnp.einsum("bsc,brc->bsr", dh, inputs, preferred_element_type=jnp.float32)
    block_sum, cross_sum = (
        lax.psum(block_part.astype(jnp.bfloat16), "dp").astype(jnp.float32),
        lax.psum(cross_part.astype(jnp.bfloat16), "dp").astype(jnp.float32),
    )
    zf = z.astype(jnp.float32)
    output = (inputs.astype(jnp.float32) + zf * gate).astype(jnp.bfloat16)
    input_grad = (cotangent.astype(jnp.float32) * (1.0 + zf * gate * (1.0 - gate)) + dv).astype(
        jnp.bfloat16
    )
    return (output, input_grad, block_sum.astype(jnp.bfloat16), cross_sum.astype(jnp.bfloat16))


def mix(
    nb, dp, rows, group,
    x_ref, b_ref, w_ref, cot_ref,
    out_ref, ig_ref, bg_ref, cg_ref,
    gate, dz, h, dz_in, h_in, dh_out, z_out, dh, z, dv,
    weight, bpart, brecv, cpart, crecv,
    send, recv, csend, crecv_sem, rsend, rrecv, gsend, grecv,
):
    me, mp = lax.axis_index("seq"), lax.axis_index("dp")
    side = nb * group
    groups = rows // group
    size, chan = x_ref.shape
    share = size // dp
    order = sorted(range(1, nb), key=lambda d: abs(d - nb / 2))

    barrier = pltpu.get_barrier_semaphore()
    for d in range(1, nb):
        pl.semaphore_signal(
            barrier, inc=1, device_id={"seq": lax.rem(me + d, nb)}, device_id_type=MESH
        )
    for e in range(1, dp):
        pl.semaphore_signal(
            barrier, inc=1, device_id={"dp": lax.rem(mp + e, dp)}, device_id_type=MESH
        )

    def exchange(k, d, src, dst, to, slot):
        return pltpu.make_async_remote_copy(
            src_ref=src.at[to],
            dst_ref=dst.at[slot],
            send_sem=send.at[k, d],
            recv_sem=recv.at[k, d],
            device_id={"seq": to},
            device_id_type=MESH,
        )

    def push(k, src, dst):
        for d in order:
            exchange(k, d, src, dst, lax.rem(me + d, nb), me).start()
        dst[me] = src[me]

    def arrived(k, d, src, dst):
        frm = lax.rem(me + nb - d, nb)
        exchange(k, d, src, dst, frm, frm).wait_recv()
        return frm

    for q in range(nb):
        at = pl.ds(q * rows, rows)
        g = jax.nn.sigmoid(x_ref[at].astype(F32))
        gate[q] = g
        dz[q] = (cot_ref[at].astype(F32) * g).astype(BF16)
    pl.semaphore_wait(barrier, nb - 1 + dp - 1)
    push(0, dz, dz_in)

    half = size // 2
    for p in range(2):
        part = jnp.dot(b_ref[p * half : (p + 1) * half], x_ref[...], preferred_element_type=F32)
        h[p * nb // 2 : (p + 1) * nb // 2] = part.astype(BF16).reshape(nb // 2, rows, chan)
    push(1, h, h_in)

    i0 = lax.broadcasted_iota(jnp.int32, (side, side), 0)
    i1 = lax.broadcasted_iota(jnp.int32, (side, side), 1)
    to_ar = jnp.where(
        (lax.rem(i0, group) == lax.div(i1, nb)) & (lax.div(i0, group) == lax.rem(i1, nb)), 1.0, 0.0
    ).astype(BF16)
    to_ra = jnp.where(
        (lax.rem(i1, group) == lax.div(i0, nb)) & (lax.div(i1, group) == lax.rem(i0, nb)), 1.0, 0.0
    ).astype(BF16)
    same = lax.rem(i0, group) == lax.rem(i1, group)
    e0 = lax.broadcasted_iota(jnp.int32, (nb, side), 0)
    e1 = lax.broadcasted_iota(jnp.int32, (nb, side), 1)
    spread = jnp.where(e0 == lax.div(e1, group), 1.0, 0.0).astype(BF16)
    w_all = w_ref[...].astype(F32)
    for g in range(groups):
        flat = w_all[g * group : (g + 1) * group].reshape(side, nb).astype(BF16)
        by_a = jnp.dot(to_ar, flat, preferred_element_type=F32).astype(BF16)
        wide = jnp.dot(by_a, spread, preferred_element_type=F32)
        weight[g] = jnp.where(same, wide, 0.0).astype(BF16)

    for d in order:
        arrived(0, d, dz, dz_in)
    for g in range(groups):
        at = pl.ds(g * group, group)
        part = lax.dot_general(
            weight[g], dz_in[:, at, :].reshape(side, chan), (((0,), (0,)), ((), ())),
            preferred_element_type=F32,
        )
        dh_out[:, at, :] = part.astype(BF16).reshape(nb, group, chan)
    push(2, dh_out, dh)

    for d in order:
        arrived(1, d, h, h_in)
    for g in range(groups):
        at = pl.ds(g * group, group)
        part = jnp.dot(
            weight[g], h_in[:, at, :].reshape(side, chan), preferred_element_type=F32
        )
        z_out[:, at, :] = part.astype(BF16).reshape(nb, group, chan)
    push(3, z_out, z)

    for g in range(groups):
        at = pl.ds(g * group, group)
        pairs = lax.dot_general(
            dz_in[:, at, :].reshape(side, chan), h_in[:, at, :].reshape(side, chan),
            (((1,), (1,)), ((), ())), preferred_element_type=F32,
        )
        kept = jnp.where(same, pairs, 0.0).astype(BF16)
        picked = lax.dot_general(
            spread, kept, (((1,), (1,)), ((), ())), preferred_element_type=F32
        )
        padded = jnp.concatenate([picked, jnp.zeros_like(picked)], axis=0)
        cpart[:, g * side : (g + 1) * side] = padded.astype(BF16)

    def share_cross(e, to, slot):
        return pltpu.make_async_remote_copy(
            src_ref=cpart,
            dst_ref=crecv.at[slot],
            send_sem=csend.at[e],
            recv_sem=crecv_sem.at[e],
            device_id={"dp": to},
            device_id_type=MESH,
        )

    for e in range(1, dp):
        share_cross(e, lax.rem(mp + e, dp), mp).start()
    crecv[mp] = cpart[...]

    for d in order:
        arrived(2, d, dh_out, dh)
    dh_all = dh[...].reshape(size, chan)
    for p in range(dp):
        part = lax.dot_general(
            dh_all[p * share : (p + 1) * share], x_ref[...], (((1,), (1,)), ((), ())),
            preferred_element_type=F32,
        )
        bpart[p] = part.astype(BF16)

    def scatter(e, to, slot):
        return pltpu.make_async_remote_copy(
            src_ref=bpart.at[to],
            dst_ref=brecv.at[slot],
            send_sem=rsend.at[e],
            recv_sem=rrecv.at[e],
            device_id={"dp": to},
            device_id_type=MESH,
        )

    for e in range(1, dp):
        scatter(e, lax.rem(mp + e, dp), mp).start()
    brecv[mp] = bpart[mp]

    third = chan // 3
    for p in range(3):
        at = slice(p * third, (p + 1) * third)
        dv[:, at] = lax.dot_general(
            b_ref[...], dh_all[:, at], (((0,), (0,)), ((), ())), preferred_element_type=F32
        )

    for e in range(1, dp):
        frm = lax.rem(mp + dp - e, dp)
        share_cross(e, frm, frm).wait_recv()
    total = crecv[0].astype(F32)
    for p in range(1, dp):
        total = total + crecv[p].astype(F32)
    total = total[:nb].astype(BF16)
    for g in range(groups):
        mine = lax.dot_general(
            to_ra, total[:, g * side : (g + 1) * side], (((1,), (1,)), ((), ())),
            preferred_element_type=F32,
        )
        cg_ref[g * group : (g + 1) * group] = mine.reshape(group, nb, nb).astype(cg_ref.dtype)

    for e in range(1, dp):
        frm = lax.rem(mp + dp - e, dp)
        scatter(e, frm, frm).wait_recv()
    summed = brecv[0].astype(F32)
    for p in range(1, dp):
        summed = summed + brecv[p].astype(F32)
    bg_ref[mp] = summed.astype(BF16)

    def gather(e, to, slot):
        return pltpu.make_async_remote_copy(
            src_ref=bg_ref.at[slot],
            dst_ref=bg_ref.at[slot],
            send_sem=gsend.at[e],
            recv_sem=grecv.at[e],
            device_id={"dp": to},
            device_id_type=MESH,
        )

    for e in range(1, dp):
        gather(e, lax.rem(mp + e, dp), mp).start()

    def finish(q):
        at = pl.ds(pl.multiple_of(q * rows, rows), rows)
        g = gate[q]
        zg = z[q].astype(F32) * g
        out_ref[at] = (x_ref[at].astype(F32) + zg).astype(BF16)
        ig_ref[at] = (
            cot_ref[at].astype(F32) * (1.0 + zg * (1.0 - g)) + dv[at]
        ).astype(BF16)

    finish(me)
    for d in order:
        finish(arrived(3, d, z_out, z))

    for e in range(1, dp):
        frm = lax.rem(mp + dp - e, dp)
        gather(e, frm, frm).wait_recv()
    for k, (src, dst) in enumerate(((dz, dz_in), (h, h_in), (dh_out, dh), (z_out, z))):
        for d in order:
            exchange(k, d, src, dst, lax.rem(me + d, nb), me).wait_send()
    for e in range(1, dp):
        to = lax.rem(mp + e, dp)
        share_cross(e, to, mp).wait_send()
        scatter(e, to, mp).wait_send()
        gather(e, to, mp).wait_send()


def fused(nb, dp, inputs, block_mix, cross_mix, cotangent):
    _, size, chan = inputs.shape
    rows = cross_mix.shape[0]
    group = 256 // nb
    side = nb * group
    groups = rows // group
    share = size // dp
    act = (nb, rows, chan)
    dma = pltpu.SemaphoreType.DMA
    flops = 6 * size * size * chan + 6 * side * side * chan * groups
    out, grad, block, cross = pl.pallas_call(
        functools.partial(mix, nb, dp, rows, group),
        out_shape=(
            jax.ShapeDtypeStruct((size, chan), BF16),
            jax.ShapeDtypeStruct((size, chan), BF16),
            jax.ShapeDtypeStruct((dp, share, size), BF16),
            jax.ShapeDtypeStruct((rows, nb, nb), BF16),
        ),
        in_specs=[pl.BlockSpec(memory_space=pltpu.VMEM)] * 4,
        out_specs=(pl.BlockSpec(memory_space=pltpu.VMEM),) * 4,
        scratch_shapes=[
            pltpu.VMEM(act, F32),
            *[pltpu.VMEM(act, BF16)] * 8,
            pltpu.VMEM((size, chan), F32),
            pltpu.VMEM((groups, side, side), BF16),
            pltpu.VMEM((dp, share, size), BF16),
            pltpu.VMEM((dp, share, size), BF16),
            pltpu.VMEM((2 * nb, rows * nb), BF16),
            pltpu.VMEM((dp, 2 * nb, rows * nb), BF16),
            dma((4, nb)),
            dma((4, nb)),
            *[dma((dp,))] * 6,
        ],
        compiler_params=pltpu.CompilerParams(
            collective_id=0, has_side_effects=True, vmem_limit_bytes=40 * 2**20
        ),
        cost_estimate=pl.CostEstimate(
            flops=flops, bytes_accessed=8 * size * chan, transcendentals=size * chan
        ),
    )(inputs.reshape(size, chan), block_mix.reshape(size, size), cross_mix,
      cotangent.reshape(size, chan))
    return (
        out.reshape(inputs.shape),
        grad.reshape(inputs.shape),
        block.reshape(block_mix.shape),
        cross,
    )


def solution(mesh):
    placed = (
        P("dp", "seq", None),
        P("seq", None, None),
        P("seq", None, None),
        P("dp", "seq", None),
    )
    nb, dp = mesh.shape["seq"], mesh.shape["dp"]

    def local(inputs, block_mix, cross_mix, cotangent):
        rows = cross_mix.shape[0]
        if nb in (8, 16) and rows % (256 // nb) == 0:
            return fused(nb, dp, inputs, block_mix, cross_mix, cotangent)
        return plain(inputs, block_mix, cross_mix, cotangent)

    return jax.shard_map(
        local,
        mesh=mesh,
        in_specs=placed,
        out_specs=(
            P("dp", "seq", None),
            P("dp", "seq", None),
            P("seq", None, None),
            P("seq", None, None),
        ),
        check_vma=False,
    )
```

```python
import functools

import jax
import jax.numpy as jnp
from jax import lax
from jax.experimental import pallas as pl
from jax.experimental.pallas import tpu as pltpu
from jax.sharding import PartitionSpec as P

MESH = pl.DeviceIdType.MESH
BF16, F32 = jnp.bfloat16, jnp.float32
VMEM_LIMIT = 63 * 2**20


def plain(inputs, block_mix, cross_mix, cotangent):
    h = jnp.einsum("bsr,brc->bsc", block_mix, inputs, preferred_element_type=jnp.float32).astype(
        jnp.bfloat16
    )
    gate = jax.nn.sigmoid(inputs.astype(jnp.float32))
    h_cols = lax.all_to_all(h, "seq", split_axis=1, concat_axis=0, tiled=True)
    z_cols = jnp.einsum(
        "rab,brc->arc", cross_mix, h_cols, preferred_element_type=jnp.float32
    ).astype(jnp.bfloat16)
    z = lax.all_to_all(z_cols, "seq", split_axis=0, concat_axis=1, tiled=True)
    dz = (cotangent.astype(jnp.float32) * gate).astype(jnp.bfloat16)
    dz_cols = lax.all_to_all(dz, "seq", split_axis=1, concat_axis=0, tiled=True)
    dh_cols = jnp.einsum(
        "rab,arc->brc", cross_mix, dz_cols, preferred_element_type=jnp.float32
    ).astype(jnp.bfloat16)
    cross_part = jnp.einsum("arc,brc->rab", dz_cols, h_cols, preferred_element_type=jnp.float32)
    dh = lax.all_to_all(dh_cols, "seq", split_axis=0, concat_axis=1, tiled=True)
    dv = jnp.einsum("bsr,bsc->brc", block_mix, dh, preferred_element_type=jnp.float32)
    block_part = jnp.einsum("bsc,brc->bsr", dh, inputs, preferred_element_type=jnp.float32)
    block_sum, cross_sum = (
        lax.psum(block_part.astype(jnp.bfloat16), "dp").astype(jnp.float32),
        lax.psum(cross_part.astype(jnp.bfloat16), "dp").astype(jnp.float32),
    )
    zf = z.astype(jnp.float32)
    output = (inputs.astype(jnp.float32) + zf * gate).astype(jnp.bfloat16)
    input_grad = (cotangent.astype(jnp.float32) * (1.0 + zf * gate * (1.0 - gate)) + dv).astype(
        jnp.bfloat16
    )
    return (output, input_grad, block_sum.astype(jnp.bfloat16), cross_sum.astype(jnp.bfloat16))


def mix(
    nb, dp, rows, group,
    x_hbm, b_hbm, w_ref, cot_hbm,
    out_hbm, ig_hbm, bg_hbm, cg_hbm,
    out_ref, ig_ref, bg_ref, cg_ref, x_ref, b_ref, cot_ref, gate, dz, h, dz_in, h_in, dh_out, z_out, dh, z, dv,
    weight, bpart, bsum, brecv, cpart, crecv,
    load, keep, send, recv, csend, crecv_sem, rsend, rrecv,
):
    me, mp = lax.axis_index("seq"), lax.axis_index("dp")
    side = nb * group
    groups = rows // group
    size, chan = x_ref.shape
    share = size // 4
    order = range(nb - 1, 0, -1)

    def partner(d):
        to, bit = 0, 1
        while bit < nb:
            to = to + bit * lax.rem(lax.div(me, bit) + (d // bit) % 2, 2)
            bit *= 2
        return to

    partners = {d: partner(d) for d in range(1, nb)}

    def span(q):
        return pl.ds(pl.multiple_of(q * rows, rows), rows)

    def loads(d, q):
        return (
            pltpu.make_async_copy(x_hbm.at[span(q)], x_ref.at[span(q)], load.at[0, d]),
            pltpu.make_async_copy(cot_hbm.at[span(q)], cot_ref.at[span(q)], load.at[1, d]),
        )

    barrier = pltpu.get_barrier_semaphore()
    for d in order:
        pl.semaphore_signal(
            barrier, inc=1, device_id={"seq": partners[d]}, device_id_type=MESH
        )
    for e in range(1, dp):
        pl.semaphore_signal(
            barrier, inc=1, device_id={"dp": lax.rem(mp + e, dp)}, device_id_type=MESH
        )
    everyone = [*((d, partners[d]) for d in order), (0, me)]
    for d, q in everyone:
        for copy in loads(d, q):
            copy.start()
    b_copy = pltpu.make_async_copy(b_hbm, b_ref, load.at[2, 0])
    b_copy.start()

    def exchange(k, d, src, dst, slot):
        return pltpu.make_async_remote_copy(
            src_ref=src.at[partners[d]],
            dst_ref=dst.at[slot],
            send_sem=send.at[k, d],
            recv_sem=recv.at[k, d],
            device_id={"seq": partners[d]},
            device_id_type=MESH,
        )

    buffers = ((dz, dz_in), (h, h_in), (dh_out, dh), (z_out, z))

    def push(k):
        for d in order:
            exchange(k, d, *buffers[k], me).start()

    def arrived(k, d):
        exchange(k, d, *buffers[k], partners[d]).wait_recv()

    for d, q in everyone:
        for copy in loads(d, q):
            copy.wait()
        g = jax.nn.sigmoid(x_ref[span(q)].astype(F32))
        gate[q] = g
        part = (cot_ref[span(q)].astype(F32) * g).astype(BF16)
        if d:
            dz[q] = part
            if d == nb - 1:
                pl.semaphore_wait(barrier, nb - 1 + dp - 1)
            exchange(0, d, dz, dz_in, me).start()
        else:
            dz_in[q] = part

    b_copy.wait()
    half = size // 2
    for p in range(2):
        part = jnp.dot(b_ref[p * half : (p + 1) * half], x_ref[...], preferred_element_type=F32)
        h[p * nb // 2 : (p + 1) * nb // 2] = part.astype(BF16).reshape(nb // 2, rows, chan)
    h_in[me] = h[me]

    i0 = lax.broadcasted_iota(jnp.int32, (side, side), 0)
    i1 = lax.broadcasted_iota(jnp.int32, (side, side), 1)
    same = lax.rem(i0, group) == lax.rem(i1, group)
    e0 = lax.broadcasted_iota(jnp.int32, (nb, side), 0)
    e1 = lax.broadcasted_iota(jnp.int32, (nb, side), 1)
    spread = jnp.where(e0 == lax.div(e1, group), 1.0, 0.0).astype(BF16)
    w_all = w_ref[...].astype(F32)
    for g in range(groups):
        lanes = jnp.concatenate(
            [w_all[:, b, g * group : (g + 1) * group] for b in range(nb)], axis=1
        ).astype(BF16)
        wide = lax.dot_general(
            spread, lanes, (((0,), (0,)), ((), ())), preferred_element_type=F32
        )
        weight[g] = jnp.where(same, wide, 0.0).astype(BF16)
    push(1)

    for d in order:
        arrived(0, d)
    for g in range(groups):
        at = pl.ds(g * group, group)
        part = lax.dot_general(
            weight[g], dz_in[:, at, :].reshape(side, chan), (((0,), (0,)), ((), ())),
            preferred_element_type=F32,
        )
        dh_out[:, at, :] = part.astype(BF16).reshape(nb, group, chan)
    dh[me] = dh_out[me]
    push(2)

    for d in order:
        arrived(1, d)
    for g in range(groups):
        at = pl.ds(g * group, group)
        part = jnp.dot(
            weight[g], h_in[:, at, :].reshape(side, chan), preferred_element_type=F32
        )
        z_out[:, at, :] = part.astype(BF16).reshape(nb, group, chan)
    z[me] = z_out[me]

    def share_cross(e, to, slot):
        return pltpu.make_async_remote_copy(
            src_ref=cpart,
            dst_ref=crecv.at[slot],
            send_sem=csend.at[e],
            recv_sem=crecv_sem.at[e],
            device_id={"dp": to},
            device_id_type=MESH,
        )

    def cross():
        for g in range(groups):
            at = pl.ds(g * group, group)
            pairs = lax.dot_general(
                dz_in[:, at, :].reshape(side, chan), h_in[:, at, :].reshape(side, chan),
                (((1,), (1,)), ((), ())), preferred_element_type=F32,
            )
            kept = jnp.where(same, pairs, 0.0).astype(BF16)
            picked = lax.dot_general(
                spread, kept, (((1,), (1,)), ((), ())), preferred_element_type=F32
            )
            padded = jnp.concatenate([picked, jnp.zeros_like(picked)], axis=0)
            cpart[:, g * side : (g + 1) * side] = padded.astype(BF16)
        for e in range(1, dp):
            share_cross(e, lax.rem(mp + e, dp), mp).start()
        crecv[mp] = cpart[...]

    push(3)

    core = lax.rem(mp, 2)
    by_core, by_x = mp + 1 - 2 * core, lax.rem(mp + 2, dp)
    top = nb // 2
    own = lax.div(me, top)

    def hop(stage, p, src, dst, to):
        return pltpu.make_async_remote_copy(
            src_ref=src,
            dst_ref=dst,
            send_sem=rsend.at[stage, p],
            recv_sem=rrecv.at[stage, p],
            device_id={"dp": to},
            device_id_type=MESH,
        )

    def hops(p, u):
        return (
            hop(0, p, bpart.at[p, 1 - core], brecv.at[0, p], by_core),
            hop(1, p, bsum.at[p], brecv.at[1, p], by_x),
            hop(2, p, bg_ref.at[u, core], bg_ref.at[u, core], by_core),
        )

    halves = tuple((p, u, hops(p, u)) for p, u in ((0, own), (1, 1 - own)))

    def half_block(p, u, hop):
        for d in order:
            if (d >= top) == (p == 1):
                arrived(2, d)
        mine = dh[pl.ds(pl.multiple_of(u * top, top), top)].reshape(half, chan)
        part = lax.dot_general(
            mine, x_ref[...], (((1,), (1,)), ((), ())), preferred_element_type=F32
        )
        bpart[p] = part.astype(BF16).reshape(2, share, size)
        hop[0].start()
        at = pl.ds(pl.multiple_of(u * half, half), half)
        third = chan // 3
        for c in range(3):
            cols = slice(c * third, (c + 1) * third)
            value = lax.dot_general(
                b_ref[at], mine[:, cols], (((0,), (0,)), ((), ())), preferred_element_type=F32
            )
            dv[:, cols] = value if p == 0 else dv[:, cols] + value

    def pair_sum(p, u, hop):
        hop[0].wait_recv()
        bsum[p] = (bpart[p, core].astype(F32) + brecv[0, p].astype(F32)).astype(BF16)
        hop[1].start()

    def full_sum(p, u, hop):
        hop[1].wait_recv()
        bg_ref[u, core] = (bsum[p].astype(F32) + brecv[1, p].astype(F32)).astype(BF16)
        hop[2].start()
        keep_block(p, 0, u, core).start()

    def keep_block(p, side, u, c):
        return pltpu.make_async_copy(bg_ref.at[u, c], bg_hbm.at[u, c], keep.at[2, 2 * p + side])

    half_block(*halves[0])
    pair_sum(*halves[0])
    cross()
    half_block(*halves[1])
    pair_sum(*halves[1])
    full_sum(*halves[0])

    for e in range(1, dp):
        frm = lax.rem(mp + dp - e, dp)
        share_cross(e, frm, frm).wait_recv()
    total = crecv[0].astype(F32)
    for p in range(1, dp):
        total = total + crecv[p].astype(F32)
    for a in range(nb):
        cg_ref[a] = jnp.concatenate(
            [
                total[:nb, g * side + a * group : g * side + (a + 1) * group]
                for g in range(groups)
            ],
            axis=1,
        ).astype(BF16)
    cg_copy = pltpu.make_async_copy(cg_ref, cg_hbm, keep.at[3, 0])
    cg_copy.start()

    def keep_rows(d, q):
        return (
            pltpu.make_async_copy(out_ref.at[span(q)], out_hbm.at[span(q)], keep.at[0, d]),
            pltpu.make_async_copy(ig_ref.at[span(q)], ig_hbm.at[span(q)], keep.at[1, d]),
        )

    def finish(d, q):
        at = span(q)
        g = gate[q]
        zg = z[q].astype(F32) * g
        out_ref[at] = (x_ref[at].astype(F32) + zg).astype(BF16)
        ig_ref[at] = (
            cot_ref[at].astype(F32) * (1.0 + zg * (1.0 - g)) + dv[at]
        ).astype(BF16)
        for copy in keep_rows(d, q):
            copy.start()

    finish(0, me)
    for d in order:
        if d < top:
            arrived(3, d)
            finish(d, partners[d])
    full_sum(*halves[1])
    for d in order:
        if d >= top:
            arrived(3, d)
            finish(d, partners[d])

    for p, u, _ in halves:
        hop(2, p, bg_ref.at[u, 1 - core], bg_ref.at[u, 1 - core], by_core).wait_recv()
        keep_block(p, 1, u, 1 - core).start()
    for k in range(4):
        for d in order:
            exchange(k, d, *buffers[k], me).wait_send()
    for e in range(1, dp):
        to = lax.rem(mp + e, dp)
        share_cross(e, to, mp).wait_send()
    for p, u, hop in halves:
        for stage in hop:
            stage.wait_send()
        keep_block(p, 0, u, core).wait()
        keep_block(p, 1, u, 1 - core).wait()
    cg_copy.wait()
    for d, q in everyone:
        for copy in keep_rows(d, q):
            copy.wait()


def store(out, grad, block, cross, out_to, grad_to, block_to, cross_to, *rest):
    *via, sems = rest
    copies = []
    arrays = ((out, out_to), (grad, grad_to), (block, block_to), (cross, cross_to))
    for i, (src, dst) in enumerate(arrays):
        pieces = 4 if i < 3 else 1
        part = src.shape[0] // pieces
        for p in range(pieces):
            at = pl.ds(p * part, part)
            copies.append((
                pltpu.make_async_copy(src.at[at], via[i].at[at], sems.at[0, i, p]),
                pltpu.make_async_copy(via[i].at[at], dst.at[at], sems.at[1, i, p]),
            ))
    for load, _ in copies:
        load.start()
    for load, keep in copies:
        load.wait()
        keep.start()
    for _, keep in copies:
        keep.wait()


def fused(nb, dp, inputs, block_mix, cross_mix, cotangent):
    _, size, chan = inputs.shape
    rows = cross_mix.shape[0]
    group = 256 // nb
    side = nb * group
    groups = rows // group
    share = size // 4
    act = (nb, rows, chan)
    dma = pltpu.SemaphoreType.DMA
    flops = 6 * size * size * chan + 6 * side * side * chan * groups
    vmem, hbm = pl.BlockSpec(memory_space=pltpu.VMEM), pl.BlockSpec(memory_space=pltpu.HBM)
    shapes = (
        jax.ShapeDtypeStruct((size, chan), BF16),
        jax.ShapeDtypeStruct((size, chan), BF16),
        jax.ShapeDtypeStruct((2, 2, share, size), BF16),
        jax.ShapeDtypeStruct((nb, nb, rows), BF16),
    )
    results = pl.pallas_call(
        functools.partial(mix, nb, dp, rows, group),
        out_shape=shapes,
        in_specs=[hbm, hbm, vmem, hbm],
        out_specs=(hbm,) * 4,
        scratch_shapes=[
            pltpu.VMEM((size, chan), BF16),
            pltpu.VMEM((size, chan), BF16),
            pltpu.VMEM((2, 2, share, size), BF16),
            pltpu.VMEM((nb, nb, rows), BF16),
            pltpu.VMEM((size, chan), BF16),
            pltpu.VMEM((size, size), BF16),
            pltpu.VMEM((size, chan), BF16),
            pltpu.VMEM(act, F32),
            *[pltpu.VMEM(act, BF16)] * 8,
            pltpu.VMEM((size, chan), F32),
            pltpu.VMEM((groups, side, side), BF16),
            pltpu.VMEM((2, 2, share, size), BF16),
            pltpu.VMEM((2, share, size), BF16),
            pltpu.VMEM((2, 2, share, size), BF16),
            pltpu.VMEM((2 * nb, rows * nb), BF16),
            pltpu.VMEM((dp, 2 * nb, rows * nb), BF16),
            dma((3, nb)),
            dma((4, max(nb, dp))),
            dma((4, nb)),
            dma((4, nb)),
            *[dma((dp,))] * 2,
            *[dma((3, 2))] * 2,
        ],
        compiler_params=pltpu.CompilerParams(
            collective_id=0, has_side_effects=True, vmem_limit_bytes=VMEM_LIMIT
        ),
        cost_estimate=pl.CostEstimate(
            flops=flops, bytes_accessed=8 * size * chan, transcendentals=size * chan
        ),
    )(inputs.reshape(size, chan), block_mix.reshape(size, size),
      cross_mix.transpose(1, 2, 0), cotangent.reshape(size, chan))
    shapes = (*shapes[:2], jax.ShapeDtypeStruct((size, size), BF16), shapes[3])
    out, grad, block, cross = pl.pallas_call(
        store,
        out_shape=shapes,
        in_specs=[hbm] * 4,
        out_specs=(hbm,) * 4,
        scratch_shapes=[*[pltpu.VMEM(a.shape, BF16) for a in shapes], dma((2, 4, 4))],
        compiler_params=pltpu.CompilerParams(vmem_limit_bytes=VMEM_LIMIT),
    )(*results[:2], results[2].reshape(shapes[2].shape), results[3])
    return (
        out.reshape(inputs.shape),
        grad.reshape(inputs.shape),
        block.reshape(block_mix.shape),
        cross.transpose(2, 0, 1),
    )


def solution(mesh):
    placed = (
        P("dp", "seq", None),
        P("seq", None, None),
        P("seq", None, None),
        P("dp", "seq", None),
    )
    nb, dp = mesh.shape["seq"], mesh.shape["dp"]

    def local(inputs, block_mix, cross_mix, cotangent):
        rows = cross_mix.shape[0]
        if nb in (8, 16) and dp == 4 and rows % (256 // nb) == 0:
            return fused(nb, dp, inputs, block_mix, cross_mix, cotangent)
        return plain(inputs, block_mix, cross_mix, cotangent)

    return jax.shard_map(
        local,
        mesh=mesh,
        in_specs=placed,
        out_specs=(
            P("dp", "seq", None),
            P("dp", "seq", None),
            P("seq", None, None),
            P("seq", None, None),
        ),
        check_vma=False,
    )
```

```python
import functools

import jax
import jax.numpy as jnp
from jax import lax
from jax.experimental import pallas as pl
from jax.experimental.pallas import tpu as pltpu
from jax.sharding import PartitionSpec as P

MESH = pl.DeviceIdType.MESH
BF16, F32 = jnp.bfloat16, jnp.float32
VMEM_LIMIT = 51 * 2**20


def plain(inputs, block_mix, cross_mix, cotangent):
    h = jnp.einsum("bsr,brc->bsc", block_mix, inputs, preferred_element_type=jnp.float32).astype(
        jnp.bfloat16
    )
    gate = jax.nn.sigmoid(inputs.astype(jnp.float32))
    h_cols = lax.all_to_all(h, "seq", split_axis=1, concat_axis=0, tiled=True)
    z_cols = jnp.einsum(
        "rab,brc->arc", cross_mix, h_cols, preferred_element_type=jnp.float32
    ).astype(jnp.bfloat16)
    z = lax.all_to_all(z_cols, "seq", split_axis=0, concat_axis=1, tiled=True)
    dz = (cotangent.astype(jnp.float32) * gate).astype(jnp.bfloat16)
    dz_cols = lax.all_to_all(dz, "seq", split_axis=1, concat_axis=0, tiled=True)
    dh_cols = jnp.einsum(
        "rab,arc->brc", cross_mix, dz_cols, preferred_element_type=jnp.float32
    ).astype(jnp.bfloat16)
    cross_part = jnp.einsum("arc,brc->rab", dz_cols, h_cols, preferred_element_type=jnp.float32)
    dh = lax.all_to_all(dh_cols, "seq", split_axis=0, concat_axis=1, tiled=True)
    dv = jnp.einsum("bsr,bsc->brc", block_mix, dh, preferred_element_type=jnp.float32)
    block_part = jnp.einsum("bsc,brc->bsr", dh, inputs, preferred_element_type=jnp.float32)
    block_sum, cross_sum = (
        lax.psum(block_part.astype(jnp.bfloat16), "dp").astype(jnp.float32),
        lax.psum(cross_part.astype(jnp.bfloat16), "dp").astype(jnp.float32),
    )
    zf = z.astype(jnp.float32)
    output = (inputs.astype(jnp.float32) + zf * gate).astype(jnp.bfloat16)
    input_grad = (cotangent.astype(jnp.float32) * (1.0 + zf * gate * (1.0 - gate)) + dv).astype(
        jnp.bfloat16
    )
    return (output, input_grad, block_sum.astype(jnp.bfloat16), cross_sum.astype(jnp.bfloat16))


def mix(
    nb, dp, rows, group,
    x_hbm, b_hbm, w_ref, cot_hbm,
    out_ref, ig_ref, bg_ref, cg_ref,
    x_ref, b_ref, cot_ref, gate, dz, h, dz_in, h_in, dh_out, z_out, dh, z, dv,
    weight, bpart, bsum, brecv, cpart, crecv,
    load, send, recv, csend, crecv_sem, rsend, rrecv,
):
    me, mp = lax.axis_index("seq"), lax.axis_index("dp")
    side = nb * group
    groups = rows // group
    size, chan = x_ref.shape
    share = size // 4
    order = range(nb - 1, 0, -1)

    def partner(d):
        to, bit = 0, 1
        while bit < nb:
            to = to + bit * lax.rem(lax.div(me, bit) + (d // bit) % 2, 2)
            bit *= 2
        return to

    partners = {d: partner(d) for d in range(1, nb)}

    def span(q):
        return pl.ds(pl.multiple_of(q * rows, rows), rows)

    def loads(d, q):
        return (
            pltpu.make_async_copy(x_hbm.at[span(q)], x_ref.at[span(q)], load.at[0, d]),
            pltpu.make_async_copy(cot_hbm.at[span(q)], cot_ref.at[span(q)], load.at[1, d]),
        )

    barrier = pltpu.get_barrier_semaphore()
    for d in order:
        pl.semaphore_signal(
            barrier, inc=1, device_id={"seq": partners[d]}, device_id_type=MESH
        )
    for e in range(1, dp):
        pl.semaphore_signal(
            barrier, inc=1, device_id={"dp": lax.rem(mp + e, dp)}, device_id_type=MESH
        )
    everyone = [*((d, partners[d]) for d in order), (0, me)]
    for d, q in everyone:
        for copy in loads(d, q):
            copy.start()
    b_copy = pltpu.make_async_copy(b_hbm, b_ref, load.at[2, 0])
    b_copy.start()

    def exchange(k, d, src, dst, slot):
        return pltpu.make_async_remote_copy(
            src_ref=src.at[partners[d]],
            dst_ref=dst.at[slot],
            send_sem=send.at[k, d],
            recv_sem=recv.at[k, d],
            device_id={"seq": partners[d]},
            device_id_type=MESH,
        )

    buffers = ((dz, dz_in), (h, h_in), (dh_out, dh), (z_out, z))

    def push(k):
        for d in order:
            exchange(k, d, *buffers[k], me).start()

    def arrived(k, d):
        exchange(k, d, *buffers[k], partners[d]).wait_recv()

    for d, q in everyone:
        for copy in loads(d, q):
            copy.wait()
        g = jax.nn.sigmoid(x_ref[span(q)].astype(F32))
        gate[q] = g
        part = (cot_ref[span(q)].astype(F32) * g).astype(BF16)
        if d:
            dz[q] = part
            if d == nb - 1:
                pl.semaphore_wait(barrier, nb - 1 + dp - 1)
            exchange(0, d, dz, dz_in, me).start()
        else:
            dz_in[q] = part

    b_copy.wait()
    half = size // 2
    for p in range(2):
        part = jnp.dot(b_ref[p * half : (p + 1) * half], x_ref[...], preferred_element_type=F32)
        h[p * nb // 2 : (p + 1) * nb // 2] = part.astype(BF16).reshape(nb // 2, rows, chan)
    h_in[me] = h[me]

    i0 = lax.broadcasted_iota(jnp.int32, (side, side), 0)
    i1 = lax.broadcasted_iota(jnp.int32, (side, side), 1)
    same = lax.rem(i0, group) == lax.rem(i1, group)
    e0 = lax.broadcasted_iota(jnp.int32, (nb, side), 0)
    e1 = lax.broadcasted_iota(jnp.int32, (nb, side), 1)
    spread = jnp.where(e0 == lax.div(e1, group), 1.0, 0.0).astype(BF16)
    w_all = w_ref[...].astype(F32)
    for g in range(groups):
        lanes = jnp.concatenate(
            [w_all[:, b, g * group : (g + 1) * group] for b in range(nb)], axis=1
        ).astype(BF16)
        wide = lax.dot_general(
            spread, lanes, (((0,), (0,)), ((), ())), preferred_element_type=F32
        )
        weight[g] = jnp.where(same, wide, 0.0).astype(BF16)
    push(1)

    for d in order:
        arrived(0, d)
    for g in range(groups):
        at = pl.ds(g * group, group)
        part = lax.dot_general(
            weight[g], dz_in[:, at, :].reshape(side, chan), (((0,), (0,)), ((), ())),
            preferred_element_type=F32,
        )
        dh_out[:, at, :] = part.astype(BF16).reshape(nb, group, chan)
    dh[me] = dh_out[me]
    push(2)

    for d in order:
        arrived(1, d)
    for g in range(groups):
        at = pl.ds(g * group, group)
        part = jnp.dot(
            weight[g], h_in[:, at, :].reshape(side, chan), preferred_element_type=F32
        )
        z_out[:, at, :] = part.astype(BF16).reshape(nb, group, chan)
    z[me] = z_out[me]

    def share_cross(e, to, slot):
        return pltpu.make_async_remote_copy(
            src_ref=cpart,
            dst_ref=crecv.at[slot],
            send_sem=csend.at[e],
            recv_sem=crecv_sem.at[e],
            device_id={"dp": to},
            device_id_type=MESH,
        )

    def cross():
        for g in range(groups):
            at = pl.ds(g * group, group)
            pairs = lax.dot_general(
                dz_in[:, at, :].reshape(side, chan), h_in[:, at, :].reshape(side, chan),
                (((1,), (1,)), ((), ())), preferred_element_type=F32,
            )
            kept = jnp.where(same, pairs, 0.0).astype(BF16)
            picked = lax.dot_general(
                spread, kept, (((1,), (1,)), ((), ())), preferred_element_type=F32
            )
            padded = jnp.concatenate([picked, jnp.zeros_like(picked)], axis=0)
            cpart[:, g * side : (g + 1) * side] = padded.astype(BF16)
        for e in range(1, dp):
            share_cross(e, lax.rem(mp + e, dp), mp).start()
        crecv[mp] = cpart[...]

    push(3)

    core = lax.rem(mp, 2)
    by_core, by_x = mp + 1 - 2 * core, lax.rem(mp + 2, dp)
    top = nb // 2
    own = lax.div(me, top)

    def hop(stage, p, src, dst, to):
        return pltpu.make_async_remote_copy(
            src_ref=src,
            dst_ref=dst,
            send_sem=rsend.at[stage, p],
            recv_sem=rrecv.at[stage, p],
            device_id={"dp": to},
            device_id_type=MESH,
        )

    def hops(p, u):
        return (
            hop(0, p, bpart.at[p, 1 - core], brecv.at[0, p], by_core),
            hop(1, p, bsum.at[p], brecv.at[1, p], by_x),
            hop(2, p, bg_ref.at[u, core], bg_ref.at[u, core], by_core),
        )

    halves = tuple((p, u, hops(p, u)) for p, u in ((0, own), (1, 1 - own)))

    def half_block(p, u, hop):
        for d in order:
            if (d >= top) == (p == 1):
                arrived(2, d)
        mine = dh[pl.ds(pl.multiple_of(u * top, top), top)].reshape(half, chan)
        part = lax.dot_general(
            mine, x_ref[...], (((1,), (1,)), ((), ())), preferred_element_type=F32
        )
        bpart[p] = part.astype(BF16).reshape(2, share, size)
        hop[0].start()
        at = pl.ds(pl.multiple_of(u * half, half), half)
        third = chan // 3
        for c in range(3):
            cols = slice(c * third, (c + 1) * third)
            value = lax.dot_general(
                b_ref[at], mine[:, cols], (((0,), (0,)), ((), ())), preferred_element_type=F32
            )
            dv[:, cols] = value if p == 0 else dv[:, cols] + value

    def pair_sum(p, u, hop):
        hop[0].wait_recv()
        bsum[p] = (bpart[p, core].astype(F32) + brecv[0, p].astype(F32)).astype(BF16)
        hop[1].start()

    def full_sum(p, u, hop):
        hop[1].wait_recv()
        bg_ref[u, core] = (bsum[p].astype(F32) + brecv[1, p].astype(F32)).astype(BF16)
        hop[2].start()

    half_block(*halves[0])
    pair_sum(*halves[0])
    cross()
    half_block(*halves[1])
    pair_sum(*halves[1])
    full_sum(*halves[0])

    for e in range(1, dp):
        frm = lax.rem(mp + dp - e, dp)
        share_cross(e, frm, frm).wait_recv()
    total = crecv[0].astype(F32)
    for p in range(1, dp):
        total = total + crecv[p].astype(F32)
    for a in range(nb):
        cg_ref[a] = jnp.concatenate(
            [
                total[:nb, g * side + a * group : g * side + (a + 1) * group]
                for g in range(groups)
            ],
            axis=1,
        ).astype(BF16)
    def finish(d, q):
        at = span(q)
        g = gate[q]
        zg = z[q].astype(F32) * g
        out_ref[at] = (x_ref[at].astype(F32) + zg).astype(BF16)
        ig_ref[at] = (
            cot_ref[at].astype(F32) * (1.0 + zg * (1.0 - g)) + dv[at]
        ).astype(BF16)

    finish(0, me)
    for d in order:
        if d < top:
            arrived(3, d)
            finish(d, partners[d])
    full_sum(*halves[1])
    for d in order:
        if d >= top:
            arrived(3, d)
            finish(d, partners[d])

    for p, u, _ in halves:
        hop(2, p, bg_ref.at[u, 1 - core], bg_ref.at[u, 1 - core], by_core).wait_recv()
    for k in range(4):
        for d in order:
            exchange(k, d, *buffers[k], me).wait_send()
    for e in range(1, dp):
        to = lax.rem(mp + e, dp)
        share_cross(e, to, mp).wait_send()
    for p, u, hop in halves:
        for stage in hop:
            stage.wait_send()


def store(out, grad, block, cross, out_to, grad_to, block_to, cross_to, sems):
    copies = []
    arrays = ((out, out_to), (grad, grad_to), (block, block_to), (cross, cross_to))
    for i, (src, dst) in enumerate(arrays):
        pieces = 4 if i < 3 else 1
        part = src.shape[0] // pieces
        for p in range(pieces):
            at = pl.ds(p * part, part)
            copies.append(pltpu.make_async_copy(src.at[at], dst.at[at], sems.at[i, p]))
    for copy in copies:
        copy.start()
    for copy in copies:
        copy.wait()


def fused(nb, dp, inputs, block_mix, cross_mix, cotangent):
    _, size, chan = inputs.shape
    rows = cross_mix.shape[0]
    group = 256 // nb
    side = nb * group
    groups = rows // group
    share = size // 4
    act = (nb, rows, chan)
    dma = pltpu.SemaphoreType.DMA
    flops = 6 * size * size * chan + 6 * side * side * chan * groups
    vmem, hbm = pl.BlockSpec(memory_space=pltpu.VMEM), pl.BlockSpec(memory_space=pltpu.HBM)
    shapes = (
        jax.ShapeDtypeStruct((size, chan), BF16),
        jax.ShapeDtypeStruct((size, chan), BF16),
        jax.ShapeDtypeStruct((2, 2, share, size), BF16),
        jax.ShapeDtypeStruct((nb, nb, rows), BF16),
    )
    results = pl.pallas_call(
        functools.partial(mix, nb, dp, rows, group),
        out_shape=shapes,
        in_specs=[hbm, hbm, vmem, hbm],
        out_specs=(vmem,) * 4,
        scratch_shapes=[
            pltpu.VMEM((size, chan), BF16),
            pltpu.VMEM((size, size), BF16),
            pltpu.VMEM((size, chan), BF16),
            pltpu.VMEM(act, F32),
            *[pltpu.VMEM(act, BF16)] * 8,
            pltpu.VMEM((size, chan), F32),
            pltpu.VMEM((groups, side, side), BF16),
            pltpu.VMEM((2, 2, share, size), BF16),
            pltpu.VMEM((2, share, size), BF16),
            pltpu.VMEM((2, 2, share, size), BF16),
            pltpu.VMEM((2 * nb, rows * nb), BF16),
            pltpu.VMEM((dp, 2 * nb, rows * nb), BF16),
            dma((3, nb)),
            dma((4, nb)),
            dma((4, nb)),
            *[dma((dp,))] * 2,
            *[dma((3, 2))] * 2,
        ],
        compiler_params=pltpu.CompilerParams(
            collective_id=0, has_side_effects=True, vmem_limit_bytes=VMEM_LIMIT
        ),
        cost_estimate=pl.CostEstimate(
            flops=flops, bytes_accessed=8 * size * chan, transcendentals=size * chan
        ),
    )(inputs.reshape(size, chan), block_mix.reshape(size, size),
      cross_mix.transpose(1, 2, 0), cotangent.reshape(size, chan))
    shapes = (*shapes[:2], jax.ShapeDtypeStruct((size, size), BF16), shapes[3])
    out, grad, block, cross = pl.pallas_call(
        store,
        out_shape=shapes,
        in_specs=[pl.BlockSpec(memory_space=pl.ANY)] * 4,
        out_specs=(hbm,) * 4,
        scratch_shapes=[dma((4, 4))],
        compiler_params=pltpu.CompilerParams(vmem_limit_bytes=2**20),
    )(*results[:2], results[2].reshape(shapes[2].shape), results[3])
    return (
        out.reshape(inputs.shape),
        grad.reshape(inputs.shape),
        block.reshape(block_mix.shape),
        cross.transpose(2, 0, 1),
    )


def solution(mesh):
    placed = (
        P("dp", "seq", None),
        P("seq", None, None),
        P("seq", None, None),
        P("dp", "seq", None),
    )
    nb, dp = mesh.shape["seq"], mesh.shape["dp"]

    def local(inputs, block_mix, cross_mix, cotangent):
        rows = cross_mix.shape[0]
        if nb in (8, 16) and dp == 4 and rows % (256 // nb) == 0:
            return fused(nb, dp, inputs, block_mix, cross_mix, cotangent)
        return plain(inputs, block_mix, cross_mix, cotangent)

    return jax.shard_map(
        local,
        mesh=mesh,
        in_specs=placed,
        out_specs=(
            P("dp", "seq", None),
            P("dp", "seq", None),
            P("seq", None, None),
            P("seq", None, None),
        ),
        check_vma=False,
    )
```

```python
import functools

import jax
import jax.numpy as jnp
from jax import lax
from jax.experimental import pallas as pl
from jax.experimental.pallas import tpu as pltpu
from jax.sharding import PartitionSpec as P

MESH = pl.DeviceIdType.MESH
BF16, F32 = jnp.bfloat16, jnp.float32
VMEM_LIMIT = 51 * 2**20


def plain(inputs, block_mix, cross_mix, cotangent):
    h = jnp.einsum("bsr,brc->bsc", block_mix, inputs, preferred_element_type=jnp.float32).astype(
        jnp.bfloat16
    )
    gate = jax.nn.sigmoid(inputs.astype(jnp.float32))
    h_cols = lax.all_to_all(h, "seq", split_axis=1, concat_axis=0, tiled=True)
    z_cols = jnp.einsum(
        "rab,brc->arc", cross_mix, h_cols, preferred_element_type=jnp.float32
    ).astype(jnp.bfloat16)
    z = lax.all_to_all(z_cols, "seq", split_axis=0, concat_axis=1, tiled=True)
    dz = (cotangent.astype(jnp.float32) * gate).astype(jnp.bfloat16)
    dz_cols = lax.all_to_all(dz, "seq", split_axis=1, concat_axis=0, tiled=True)
    dh_cols = jnp.einsum(
        "rab,arc->brc", cross_mix, dz_cols, preferred_element_type=jnp.float32
    ).astype(jnp.bfloat16)
    cross_part = jnp.einsum("arc,brc->rab", dz_cols, h_cols, preferred_element_type=jnp.float32)
    dh = lax.all_to_all(dh_cols, "seq", split_axis=0, concat_axis=1, tiled=True)
    dv = jnp.einsum("bsr,bsc->brc", block_mix, dh, preferred_element_type=jnp.float32)
    block_part = jnp.einsum("bsc,brc->bsr", dh, inputs, preferred_element_type=jnp.float32)
    block_sum, cross_sum = (
        lax.psum(block_part.astype(jnp.bfloat16), "dp").astype(jnp.float32),
        lax.psum(cross_part.astype(jnp.bfloat16), "dp").astype(jnp.float32),
    )
    zf = z.astype(jnp.float32)
    output = (inputs.astype(jnp.float32) + zf * gate).astype(jnp.bfloat16)
    input_grad = (cotangent.astype(jnp.float32) * (1.0 + zf * gate * (1.0 - gate)) + dv).astype(
        jnp.bfloat16
    )
    return (output, input_grad, block_sum.astype(jnp.bfloat16), cross_sum.astype(jnp.bfloat16))


def mix(
    nb, dp, rows, group,
    x_hbm, b_hbm, w_ref, cot_hbm,
    out_ref, ig_ref, bg_ref, cg_ref,
    x_ref, b_ref, cot_ref, gate, dz, h, dz_in, h_in, dh_out, z_out, dh, z, dv,
    weight, bpart, bsum, brecv, cpart, crecv,
    load, send, recv, csend, crecv_sem, rsend, rrecv,
):
    me, mp = lax.axis_index("seq"), lax.axis_index("dp")
    side = nb * group
    groups = rows // group
    size, chan = x_ref.shape
    share = size // 4
    far = nb // 2
    order = [*range(far + far // 2 - 1, far - 1, -1), *range(nb - 1, far + far // 2 - 1, -1), *range(far - 1, 0, -1)]

    def partner(d):
        to, bit = 0, 1
        while bit < nb:
            to = to + bit * lax.rem(lax.div(me, bit) + (d // bit) % 2, 2)
            bit *= 2
        return to

    partners = {d: partner(d) for d in range(1, nb)}

    def span(q):
        return pl.ds(pl.multiple_of(q * rows, rows), rows)

    def loads(d, q):
        return (
            pltpu.make_async_copy(x_hbm.at[span(q)], x_ref.at[span(q)], load.at[0, d]),
            pltpu.make_async_copy(cot_hbm.at[span(q)], cot_ref.at[span(q)], load.at[1, d]),
        )

    barrier = pltpu.get_barrier_semaphore()
    for d in order:
        pl.semaphore_signal(
            barrier, inc=1, device_id={"seq": partners[d]}, device_id_type=MESH
        )
    for e in range(1, dp):
        pl.semaphore_signal(
            barrier, inc=1, device_id={"dp": lax.rem(mp + e, dp)}, device_id_type=MESH
        )
    everyone = [*((d, partners[d]) for d in order), (0, me)]
    for d, q in everyone:
        for copy in loads(d, q):
            copy.start()
    b_copy = pltpu.make_async_copy(b_hbm, b_ref, load.at[2, 0])
    b_copy.start()

    def exchange(k, d, src, dst, slot):
        return pltpu.make_async_remote_copy(
            src_ref=src.at[partners[d]],
            dst_ref=dst.at[slot],
            send_sem=send.at[k, d],
            recv_sem=recv.at[k, d],
            device_id={"seq": partners[d]},
            device_id_type=MESH,
        )

    buffers = ((dz, dz_in), (h, h_in), (dh_out, dh), (z_out, z))

    def push(k):
        for d in order:
            exchange(k, d, *buffers[k], me).start()

    def arrived(k, d):
        exchange(k, d, *buffers[k], partners[d]).wait_recv()

    for d, q in everyone:
        for copy in loads(d, q):
            copy.wait()
        g = jax.nn.sigmoid(x_ref[span(q)].astype(F32))
        gate[q] = g
        part = (cot_ref[span(q)].astype(F32) * g).astype(BF16)
        if d:
            dz[q] = part
            if d == order[0]:
                pl.semaphore_wait(barrier, nb - 1 + dp - 1)
            exchange(0, d, dz, dz_in, me).start()
        else:
            dz_in[q] = part

    b_copy.wait()
    half = size // 2
    for p in range(2):
        part = jnp.dot(b_ref[p * half : (p + 1) * half], x_ref[...], preferred_element_type=F32)
        h[p * nb // 2 : (p + 1) * nb // 2] = part.astype(BF16).reshape(nb // 2, rows, chan)
    h_in[me] = h[me]

    i0 = lax.broadcasted_iota(jnp.int32, (side, side), 0)
    i1 = lax.broadcasted_iota(jnp.int32, (side, side), 1)
    same = lax.rem(i0, group) == lax.rem(i1, group)
    e0 = lax.broadcasted_iota(jnp.int32, (nb, side), 0)
    e1 = lax.broadcasted_iota(jnp.int32, (nb, side), 1)
    spread = jnp.where(e0 == lax.div(e1, group), 1.0, 0.0).astype(BF16)
    w_all = w_ref[...].astype(F32)
    for g in range(groups):
        lanes = jnp.concatenate(
            [w_all[:, b, g * group : (g + 1) * group] for b in range(nb)], axis=1
        ).astype(BF16)
        wide = lax.dot_general(
            spread, lanes, (((0,), (0,)), ((), ())), preferred_element_type=F32
        )
        weight[g] = jnp.where(same, wide, 0.0).astype(BF16)
    push(1)

    for d in order:
        arrived(0, d)
    for g in range(groups):
        at = pl.ds(g * group, group)
        part = lax.dot_general(
            weight[g], dz_in[:, at, :].reshape(side, chan), (((0,), (0,)), ((), ())),
            preferred_element_type=F32,
        )
        dh_out[:, at, :] = part.astype(BF16).reshape(nb, group, chan)
    dh[me] = dh_out[me]
    push(2)

    for d in order:
        arrived(1, d)
    for g in range(groups):
        at = pl.ds(g * group, group)
        part = jnp.dot(
            weight[g], h_in[:, at, :].reshape(side, chan), preferred_element_type=F32
        )
        z_out[:, at, :] = part.astype(BF16).reshape(nb, group, chan)
    z[me] = z_out[me]

    def share_cross(e, to, slot):
        return pltpu.make_async_remote_copy(
            src_ref=cpart,
            dst_ref=crecv.at[slot],
            send_sem=csend.at[e],
            recv_sem=crecv_sem.at[e],
            device_id={"dp": to},
            device_id_type=MESH,
        )

    def cross():
        for g in range(groups):
            at = pl.ds(g * group, group)
            pairs = lax.dot_general(
                dz_in[:, at, :].reshape(side, chan), h_in[:, at, :].reshape(side, chan),
                (((1,), (1,)), ((), ())), preferred_element_type=F32,
            )
            kept = jnp.where(same, pairs, 0.0).astype(BF16)
            picked = lax.dot_general(
                spread, kept, (((1,), (1,)), ((), ())), preferred_element_type=F32
            )
            padded = jnp.concatenate([picked, jnp.zeros_like(picked)], axis=0)
            cpart[:, g * side : (g + 1) * side] = padded.astype(BF16)
        for e in range(1, dp):
            share_cross(e, lax.rem(mp + e, dp), mp).start()
        crecv[mp] = cpart[...]

    push(3)

    core = lax.rem(mp, 2)
    by_core, by_x = mp + 1 - 2 * core, lax.rem(mp + 2, dp)
    top = nb // 2
    own = lax.div(me, top)

    def hop(stage, p, src, dst, to):
        return pltpu.make_async_remote_copy(
            src_ref=src,
            dst_ref=dst,
            send_sem=rsend.at[stage, p],
            recv_sem=rrecv.at[stage, p],
            device_id={"dp": to},
            device_id_type=MESH,
        )

    def hops(p, u):
        return (
            hop(0, p, bpart.at[p, 1 - core], brecv.at[0, p], by_core),
            hop(1, p, bsum.at[p], brecv.at[1, p], by_x),
            hop(2, p, bg_ref.at[u, core], bg_ref.at[u, core], by_core),
        )

    halves = tuple((p, u, hops(p, u)) for p, u in ((0, own), (1, 1 - own)))

    def half_block(p, u, hop):
        for d in order:
            if (d >= top) == (p == 1):
                arrived(2, d)
        mine = dh[pl.ds(pl.multiple_of(u * top, top), top)].reshape(half, chan)
        part = lax.dot_general(
            mine, x_ref[...], (((1,), (1,)), ((), ())), preferred_element_type=F32
        )
        bpart[p] = part.astype(BF16).reshape(2, share, size)
        hop[0].start()
        at = pl.ds(pl.multiple_of(u * half, half), half)
        third = chan // 3
        for c in range(3):
            cols = slice(c * third, (c + 1) * third)
            value = lax.dot_general(
                b_ref[at], mine[:, cols], (((0,), (0,)), ((), ())), preferred_element_type=F32
            )
            dv[:, cols] = value if p == 0 else dv[:, cols] + value

    def pair_sum(p, u, hop):
        hop[0].wait_recv()
        bsum[p] = (bpart[p, core].astype(F32) + brecv[0, p].astype(F32)).astype(BF16)
        hop[1].start()

    def full_sum(p, u, hop):
        hop[1].wait_recv()
        bg_ref[u, core] = (bsum[p].astype(F32) + brecv[1, p].astype(F32)).astype(BF16)
        hop[2].start()

    half_block(*halves[0])
    pair_sum(*halves[0])
    cross()
    half_block(*halves[1])
    pair_sum(*halves[1])
    full_sum(*halves[0])

    for e in range(1, dp):
        frm = lax.rem(mp + dp - e, dp)
        share_cross(e, frm, frm).wait_recv()
    total = crecv[0].astype(F32)
    for p in range(1, dp):
        total = total + crecv[p].astype(F32)
    for a in range(nb):
        cg_ref[a] = jnp.concatenate(
            [
                total[:nb, g * side + a * group : g * side + (a + 1) * group]
                for g in range(groups)
            ],
            axis=1,
        ).astype(BF16)
    def finish(d, q):
        at = span(q)
        g = gate[q]
        zg = z[q].astype(F32) * g
        out_ref[at] = (x_ref[at].astype(F32) + zg).astype(BF16)
        ig_ref[at] = (
            cot_ref[at].astype(F32) * (1.0 + zg * (1.0 - g)) + dv[at]
        ).astype(BF16)

    finish(0, me)
    for d in order:
        if d < top:
            arrived(3, d)
            finish(d, partners[d])
    full_sum(*halves[1])
    for d in order:
        if d >= top:
            arrived(3, d)
            finish(d, partners[d])

    for p, u, _ in halves:
        hop(2, p, bg_ref.at[u, 1 - core], bg_ref.at[u, 1 - core], by_core).wait_recv()
    for k in range(4):
        for d in order:
            exchange(k, d, *buffers[k], me).wait_send()
    for e in range(1, dp):
        to = lax.rem(mp + e, dp)
        share_cross(e, to, mp).wait_send()
    for p, u, hop in halves:
        for stage in hop:
            stage.wait_send()


def store(out, grad, block, cross, out_to, grad_to, block_to, cross_to, sems):
    copies = []
    arrays = ((out, out_to), (grad, grad_to), (block, block_to), (cross, cross_to))
    for i, (src, dst) in enumerate(arrays):
        pieces = 4 if i < 3 else 1
        part = src.shape[0] // pieces
        for p in range(pieces):
            at = pl.ds(p * part, part)
            copies.append(pltpu.make_async_copy(src.at[at], dst.at[at], sems.at[i, p]))
    for copy in copies:
        copy.start()
    for copy in copies:
        copy.wait()


def fused(nb, dp, inputs, block_mix, cross_mix, cotangent):
    _, size, chan = inputs.shape
    rows = cross_mix.shape[0]
    group = 256 // nb
    side = nb * group
    groups = rows // group
    share = size // 4
    act = (nb, rows, chan)
    dma = pltpu.SemaphoreType.DMA
    flops = 6 * size * size * chan + 6 * side * side * chan * groups
    vmem, hbm = pl.BlockSpec(memory_space=pltpu.VMEM), pl.BlockSpec(memory_space=pltpu.HBM)
    shapes = (
        jax.ShapeDtypeStruct((size, chan), BF16),
        jax.ShapeDtypeStruct((size, chan), BF16),
        jax.ShapeDtypeStruct((2, 2, share, size), BF16),
        jax.ShapeDtypeStruct((nb, nb, rows), BF16),
    )
    results = pl.pallas_call(
        functools.partial(mix, nb, dp, rows, group),
        out_shape=shapes,
        in_specs=[hbm, hbm, vmem, hbm],
        out_specs=(vmem,) * 4,
        scratch_shapes=[
            pltpu.VMEM((size, chan), BF16),
            pltpu.VMEM((size, size), BF16),
            pltpu.VMEM((size, chan), BF16),
            pltpu.VMEM(act, F32),
            *[pltpu.VMEM(act, BF16)] * 8,
            pltpu.VMEM((size, chan), F32),
            pltpu.VMEM((groups, side, side), BF16),
            pltpu.VMEM((2, 2, share, size), BF16),
            pltpu.VMEM((2, share, size), BF16),
            pltpu.VMEM((2, 2, share, size), BF16),
            pltpu.VMEM((2 * nb, rows * nb), BF16),
            pltpu.VMEM((dp, 2 * nb, rows * nb), BF16),
            dma((3, nb)),
            dma((4, nb)),
            dma((4, nb)),
            *[dma((dp,))] * 2,
            *[dma((3, 2))] * 2,
        ],
        compiler_params=pltpu.CompilerParams(
            collective_id=0, has_side_effects=True, vmem_limit_bytes=VMEM_LIMIT
        ),
        cost_estimate=pl.CostEstimate(
            flops=flops, bytes_accessed=8 * size * chan, transcendentals=size * chan
        ),
    )(inputs.reshape(size, chan), block_mix.reshape(size, size),
      cross_mix.transpose(1, 2, 0), cotangent.reshape(size, chan))
    shapes = (*shapes[:2], jax.ShapeDtypeStruct((size, size), BF16), shapes[3])
    out, grad, block, cross = pl.pallas_call(
        store,
        out_shape=shapes,
        in_specs=[pl.BlockSpec(memory_space=pl.ANY)] * 4,
        out_specs=(hbm,) * 4,
        scratch_shapes=[dma((4, 4))],
        compiler_params=pltpu.CompilerParams(vmem_limit_bytes=2**20),
    )(*results[:2], results[2].reshape(shapes[2].shape), results[3])
    return (
        out.reshape(inputs.shape),
        grad.reshape(inputs.shape),
        block.reshape(block_mix.shape),
        cross.transpose(2, 0, 1),
    )


def solution(mesh):
    placed = (
        P("dp", "seq", None),
        P("seq", None, None),
        P("seq", None, None),
        P("dp", "seq", None),
    )
    nb, dp = mesh.shape["seq"], mesh.shape["dp"]

    def local(inputs, block_mix, cross_mix, cotangent):
        rows = cross_mix.shape[0]
        if nb in (8, 16) and dp == 4 and rows % (256 // nb) == 0:
            return fused(nb, dp, inputs, block_mix, cross_mix, cotangent)
        return plain(inputs, block_mix, cross_mix, cotangent)

    return jax.shard_map(
        local,
        mesh=mesh,
        in_specs=placed,
        out_specs=(
            P("dp", "seq", None),
            P("dp", "seq", None),
            P("seq", None, None),
            P("seq", None, None),
        ),
        check_vma=False,
    )
```
